32 devices in a mesh: section: 4 (over y, x), ctx: 8 (over z, core).
Axes of the slice: x: 2, y: 2, z: 4, core: 2. Of those that a mesh axis runs over, the one named last changes fastest.
Arguments:
- acts: bfloat16 [4, 1024, 12288], P('section', 'ctx'), may hold values from -6 to 6
- cots: bfloat16 [4, 1024, 4096], P('section', 'ctx'), may hold values from -1.1953125 to 1.1953125
- kern: float32 [4, 7, 12288], P('section'), may hold values from -2 to 2
- filt: bfloat16 [4, 4096, 1024], P('section', 'ctx'), may hold values from -9 to 9
- skip: float32 [4, 4096], P('section'), may hold values from 0.5 to 1.5
Outputs:
- output: bfloat16 [4, 1024, 4096], P('section', 'ctx')
- input_grad: bfloat16 [4, 1024, 12288], P('section', 'ctx')
- kern_grad: float32 [4, 7, 12288], P('section')
- filt_grad: float32 [4, 4096, 1024], P('section', 'ctx')
- skip_grad: float32 [4, 4096], P('section', 'ctx')
The draws below stay inside these ranges and needn't reach their ends.
All inputs are finite; a program needn't handle non-finite values.
Results may differ from the reference program's by a relative error of at most 0.023.
Values may be sent and summed in bfloat16 or wider, within the bound.
A program may use at most 192 MiB of HBM per device.

```python
import math
import jax
import jax.numpy as jnp
from jax import lax

D = 4096
TAPS = 7
SECTIONS = 4
SEQ = 1024
FEATS = 12288


def draw_filt(key, part):
    key_rate = jax.random.fold_in(key, 11)
    key_noise = jax.random.fold_in(key, 12)
    lower, upper = (0.5, 50.0)
    rates = jnp.exp(jax.random.uniform(key_rate, (SECTIONS, D, 1), jnp.float32, math.log(lower), math.log(upper)))
    places = jnp.arange(SEQ, dtype=jnp.float32)[None, None, :] / SEQ
    envelope = jnp.sqrt(2.0 * rates / SEQ) * jnp.exp(-rates * places)
    noise = jnp.clip(jax.random.normal(key_noise, (SECTIONS, D, SEQ), jnp.float32), -4.0, 4.0)
    return (noise * envelope).astype(jnp.bfloat16)


def steps_of(stream_key, extent, pieces, smallest, largest):
    def one(position, blocks):
        heights = jax.random.uniform(jax.random.fold_in(jax.random.fold_in(stream_key, 6), position), (blocks,), jnp.float32, smallest / len(pieces), largest / len(pieces))
        return jnp.repeat(jnp.exp(heights), extent[position] // blocks).reshape((-1,) + (1,) * (len(extent) - position - 1))

    loudness = one(*pieces[0])
    for cut in pieces[1:]:
        loudness = loudness * one(*cut)
    return loudness


def bell_draw(rng, shape, width, bound, shards=(), held_as=jnp.bfloat16):
    loudness = steps_of(rng, shape, shards, -0.22, 0.18) if shards else 1.0
    array = jax.random.normal(rng, shape, jnp.float32) * width * loudness
    return jnp.minimum(jnp.maximum(array, -bound), bound).astype(held_as)


def setup_inputs(seed: int = 0) -> dict:
    arg_keys = jax.random.split(jax.random.key(seed), 6)
    return {
        "acts": bell_draw(arg_keys[0], (SECTIONS, SEQ, FEATS), 1.0, 6.0, ((0, 4), (1, 8))),
        "cots": bell_draw(arg_keys[1], (SECTIONS, SEQ, D), 0.2, 1.1953125, ((0, 4), (1, 8))),
        "kern": bell_draw(arg_keys[2], (SECTIONS, TAPS, FEATS), TAPS ** -0.5, 2.0, ((0, 4),), jnp.float32),
        "filt": draw_filt(jax.random.fold_in(arg_keys[5], 71), 0),
        "skip": jnp.clip(0.5 + 1.0 * jax.random.uniform(arg_keys[4], (SECTIONS, D), jnp.float32) ** steps_of(arg_keys[4], (SECTIONS, D), ((0, 4),), -0.2, 0.2), 0.5, 1.5),
    }


def causal_conv(signal, taps_f):
    length = signal.shape[0]
    spec = jnp.fft.rfft(signal, n=2 * length, axis=0) * jnp.fft.rfft(taps_f, n=2 * length, axis=0)
    return jnp.fft.irfft(spec, n=2 * length, axis=0)[:length]


def correlate(signal, taps_f):
    length = signal.shape[0]
    spec = jnp.fft.rfft(signal, n=2 * length, axis=0) * jnp.conj(jnp.fft.rfft(taps_f, n=2 * length, axis=0))
    return jnp.fft.irfft(spec, n=2 * length, axis=0)[:length]


def one_section(item):
    source, incoming, weights, filter_row, gain = item
    length = source.shape[0]
    margin = TAPS - 1
    padded = jnp.pad(source.astype(jnp.float32), ((margin, 0), (0, 0)))
    feature = sum(weights[offset][None, :] * padded[margin - offset:margin - offset + length] for offset in range(TAPS))
    query = feature[:, :D]
    keyed = feature[:, D:2 * D]
    value = feature[:, 2 * D:]
    gated = lax.optimization_barrier((keyed * value).astype(jnp.bfloat16)).astype(jnp.float32)
    taps_f = filter_row.astype(jnp.float32).T
    mixed = lax.optimization_barrier(causal_conv(gated, taps_f).astype(jnp.bfloat16)).astype(jnp.float32)
    inner = mixed + gain[None, :] * gated
    output = (query * inner).astype(jnp.bfloat16)
    grad_f = incoming.astype(jnp.float32)
    grad_mix = lax.optimization_barrier((grad_f * query).astype(jnp.bfloat16)).astype(jnp.float32)
    through = lax.optimization_barrier((correlate(grad_mix, taps_f) + gain[None, :] * grad_mix).astype(jnp.bfloat16)).astype(jnp.float32)
    filt_grad = correlate(grad_mix, gated).T
    skip_grad = jnp.sum(grad_mix * gated, axis=0)
    feat_grad = jnp.concatenate([grad_f * inner, through * value, through * keyed], axis=1)
    kern_grad = jnp.stack([jnp.sum(feat_grad * padded[margin - offset:margin - offset + length], axis=0) for offset in range(TAPS)])
    extended = jnp.pad(feat_grad, ((0, margin), (0, 0)))
    input_grad = sum(weights[offset][None, :] * extended[offset:offset + length] for offset in range(TAPS)).astype(jnp.bfloat16)
    return output, input_grad, kern_grad, filt_grad, skip_grad


def reference(acts, cots, kern, filt, skip):
    sources = jnp.roll(acts, 1, axis=0)
    incoming = jnp.roll(cots, -1, axis=0)
    output, input_grad, kern_grad, filt_grad, skip_grad = lax.map(one_section, (sources, incoming, kern, filt, skip))
    return (output, input_grad, kern_grad, filt_grad, skip_grad)
```

```python
import functools

import jax
import jax.numpy as jnp
import ml_dtypes
import numpy as np
from jax import lax
from jax.experimental import pallas as pl
from jax.experimental.pallas import tpu as pltpu
from jax.sharding import PartitionSpec as P

MESH = pl.DeviceIdType.MESH
LANES = 128
HALO = 16
F32 = jnp.float32
BF16 = jnp.bfloat16


def make_tables(length):
    half = 2 * np.arange(length, dtype=np.int64) + 1
    angle = (np.outer(half, half) % (8 * length)) * (2.0 * np.pi / (8 * length))
    phase = half * (np.pi / (4 * length))
    twist = np.stack([np.cos(phase), np.sin(phase)]).astype(np.float32)
    twist = np.ascontiguousarray(np.broadcast_to(twist[:, :, None], (2, length, LANES)))
    return (
        np.cos(angle).astype(ml_dtypes.bfloat16),
        np.sin(angle).astype(ml_dtypes.bfloat16),
        twist,
    )


def kernel(
    sections, groups, chunks,
    acts, cots, kern, filt, skip, c4, s4, twist,
    out, igrad, kgrad, fgrad, sgrad,
    srcv, incv, hst, hrx, gst, grx, stg, gx, rx, xf, fgb, fsp, prod, kst, krx, ksum, kall,
    src_send, src_recv, inc_send, inc_recv, h_send, h_recv, g_send, g_recv,
    x_send, x_recv, r_send, r_recv, ks_send, ks_recv, ka_send, ka_recv, o_sem, i_sem,
):
    sec = lax.axis_index("section")
    me = lax.axis_index("ctx")
    tokens, width = cots.shape
    chans = width // groups
    taps = kern.shape[0]
    length = c4.shape[0]
    rows_step = 256
    after_sec = lax.rem(sec + 1, sections)
    before_sec = lax.rem(sec + sections - 1, sections)

    barrier = pltpu.get_barrier_semaphore()
    pl.semaphore_signal(barrier, inc=1, device_id={"section": after_sec}, device_id_type=MESH)
    pl.semaphore_signal(barrier, inc=1, device_id={"section": before_sec}, device_id_type=MESH)
    for step in range(1, groups):
        pl.semaphore_signal(
            barrier, inc=1, device_id={"ctx": lax.rem(me + step, groups)}, device_id_type=MESH
        )
    pl.semaphore_wait(barrier, groups + 1)

    def column(part, group, k):
        return pl.multiple_of(part * width + group * chans + k * LANES, LANES)

    def remote(src, dst, send, recv, where):
        return pltpu.make_async_remote_copy(
            src_ref=src, dst_ref=dst, send_sem=send, recv_sem=recv,
            device_id=where, device_id_type=MESH,
        )

    def drain(ref, sem):
        pltpu.make_async_copy(ref, ref, sem).wait()

    def hand_on(k):
        def body(group, carry):
            for part in range(3):
                remote(
                    acts.at[:, pl.ds(column(part, group, k), LANES)],
                    srcv.at[k, part * groups + group],
                    src_send.at[k], src_recv.at[k], {"section": after_sec},
                ).start()
            remote(
                cots.at[:, pl.ds(column(0, group, k), LANES)],
                incv.at[k, group],
                inc_send.at[k], inc_recv.at[k], {"section": before_sec},
            ).start()
            return carry

        lax.fori_loop(0, groups, body, 0)

    def to_peers(make):
        def body(step, carry):
            make(lax.rem(me + step, groups)).start()
            return carry

        lax.fori_loop(1, groups, body, 0)

    def features(k, group):
        result = []
        for part in range(3):
            strip = part * groups + group
            xf[part, :HALO, :] = hrx[k, strip].astype(F32)
            xf[part, HALO:, :] = srcv[k, strip].astype(F32)
            columns = pl.ds(column(part, group, k), LANES)
            total = None
            for j in range(taps):
                term = kern[j : j + 1, columns] * xf[part, pl.ds(HALO - j, tokens), :]
                total = term if total is None else total + term
            result.append(total)
        return result

    hand_on(0)
    if chunks > 1:
        hand_on(1)

    @pl.loop(0, length // rows_step)
    def _(r):
        rows = pl.ds(pl.multiple_of(r * rows_step, rows_step), rows_step)
        dims = (((1,), (1,)), ((), ()))
        c = lax.dot_general(c4[rows, :], filt[...], dims, preferred_element_type=F32)
        s = lax.dot_general(s4[rows, :], filt[...], dims, preferred_element_type=F32)
        tc = twist[0, rows, :]
        ts = twist[1, rows, :]
        for k in range(chunks):
            ck = c[:, k * LANES : (k + 1) * LANES]
            sk = s[:, k * LANES : (k + 1) * LANES]
            fsp[0, k, rows, :] = (ck * tc + sk * ts).astype(BF16)
            fsp[1, k, rows, :] = (sk * tc - ck * ts).astype(BF16)

    def stage_a(k):
        drain(srcv.at[k], src_recv.at[k])
        if k + 2 < chunks:
            drain(srcv.at[k], src_send.at[k])
            drain(incv.at[k], inc_send.at[k])
            hand_on(k + 2)

        @pl.loop(0, 3 * groups)
        def _(strip):
            hst[k, strip] = srcv[k, strip, tokens - HALO :, :]

        @pl.when(me < groups - 1)
        def _():
            remote(hst.at[k], hrx.at[k], h_send.at[k], h_recv.at[k], {"ctx": me + 1}).start()

        drain(incv.at[k], inc_recv.at[k])

        @pl.when(me > 0)
        def _():
            drain(hrx.at[k], h_recv.at[k])

        @pl.when(me == 0)
        def _():
            hrx[k] = jnp.zeros(hrx.shape[1:], BF16)

        @pl.loop(0, groups)
        def _(group):
            query, keyed, value = features(k, group)
            stg[k, group, :, :LANES] = (keyed * value).astype(BF16)
            stg[k, group, :, LANES:] = (incv[k, group].astype(F32) * query).astype(BF16)

        mine = pl.ds(pl.multiple_of(me * tokens, tokens), tokens)
        to_peers(
            lambda peer: remote(
                stg.at[k, peer], gx.at[k, mine, :], x_send.at[k], x_recv.at[k], {"ctx": peer}
            )
        )
        gx[k, mine, :] = stg[k, me]

    def stage_c(k):
        drain(gx.at[k, pl.ds(0, (groups - 1) * tokens), :], x_recv.at[k])

        @pl.loop(0, length // rows_step)
        def _(r):
            rows = pl.ds(pl.multiple_of(r * rows_step, rows_step), rows_step)
            x = gx[k]
            c = jnp.dot(c4[rows, :], x, preferred_element_type=F32)
            s = jnp.dot(s4[rows, :], x, preferred_element_type=F32)
            cg, cm = c[:, :LANES], c[:, LANES:]
            sg, sm = s[:, :LANES], s[:, LANES:]
            fc = fsp[0, k, rows, :].astype(F32)
            fs = fsp[1, k, rows, :].astype(F32)
            prod[0, rows, :LANES] = (cg * fc - sg * fs).astype(BF16)
            prod[1, rows, :LANES] = (cg * fs + sg * fc).astype(BF16)
            prod[0, rows, LANES : 2 * LANES] = (cm * fc + sm * fs).astype(BF16)
            prod[1, rows, LANES : 2 * LANES] = (sm * fc - cm * fs).astype(BF16)
            uc = cm * cg + sm * sg
            us = sm * cg - cm * sg
            tc = twist[0, rows, :]
            ts = twist[1, rows, :]
            prod[0, rows, 2 * LANES :] = (uc * tc - us * ts).astype(BF16)
            prod[1, rows, 2 * LANES :] = (uc * ts + us * tc).astype(BF16)

        gain = skip[:, pl.ds(pl.multiple_of(me * chans + k * LANES, LANES), LANES)]

        def back(r, total):
            start = pl.multiple_of(r * rows_step, rows_step)
            rows = pl.ds(start, rows_step)
            y = jnp.dot(c4[rows, :], prod[0], preferred_element_type=F32)
            y = y + jnp.dot(s4[rows, :], prod[1], preferred_element_type=F32)
            y = y * (1.0 / length)
            gated = gx[k, rows, :LANES].astype(F32)
            grad = gx[k, rows, LANES:].astype(F32)
            gx[k, rows, :LANES] = y[:, :LANES].astype(BF16)
            gx[k, rows, LANES:] = (y[:, LANES : 2 * LANES] + gain * grad).astype(BF16)
            fgrad[k * LANES : (k + 1) * LANES, rows] = y[:, 2 * LANES :].T
            return total + jnp.sum(gated * grad, axis=0, keepdims=True)

        sgrad[:, k * LANES : (k + 1) * LANES] = lax.fori_loop(
            0, length // rows_step, back, jnp.zeros((1, LANES), F32)
        )
        to_peers(
            lambda peer: remote(
                gx.at[k, pl.ds(pl.multiple_of(peer * tokens, tokens), tokens), :],
                rx.at[k, me],
                r_send.at[k], r_recv.at[k], {"ctx": peer},
            )
        )
        rx[k, me] = gx[k, pl.ds(pl.multiple_of(me * tokens, tokens), tokens), :]

    def stage_d(k):
        drain(rx.at[k, pl.ds(0, groups - 1)], r_recv.at[k])
        drain(stg.at[k, pl.ds(0, groups - 1)], x_send.at[k])

        @pl.loop(0, groups)
        def _(group):
            query, keyed, value = features(k, group)
            gain = skip[:, pl.ds(column(0, group, k), LANES)]
            mixed = rx[k, group, :, :LANES].astype(F32)
            through = rx[k, group, :, LANES:].astype(F32)
            inner = mixed + gain * stg[k, group, :, :LANES].astype(F32)
            stg[k, group, :, :LANES] = (query * inner).astype(BF16)
            pltpu.make_async_copy(
                stg.at[k, group, :, pl.ds(0, LANES)],
                out.at[:, pl.ds(column(0, group, k), LANES)],
                o_sem.at[k],
            ).start()
            grads = (incv[k, group].astype(F32) * inner, through * value, through * keyed)
            for part in range(3):
                strip = part * groups + group
                grad = grads[part]
                fgb[strip, :tokens, :] = grad
                gst[k, strip] = grad[:HALO].astype(BF16)
                for j in range(taps):
                    kst[k, group, part, j : j + 1, :] = jnp.sum(
                        grad * xf[part, pl.ds(HALO - j, tokens), :], axis=0, keepdims=True
                    )
                kst[k, group, part, taps:, :] = jnp.zeros((8 - taps, LANES), F32)

        @pl.when(me > 0)
        def _():
            remote(gst.at[k], grx.at[k], g_send.at[k], g_recv.at[k], {"ctx": me - 1}).start()

        to_peers(
            lambda peer: remote(
                kst.at[k, peer], krx.at[k, me], ks_send.at[k], ks_recv.at[k], {"ctx": peer}
            )
        )
        krx[k, me] = kst[k, me]
        drain(krx.at[k, pl.ds(0, groups - 1)], ks_recv.at[k])
        total = krx[k, 0]
        for group in range(1, groups):
            total = total + krx[k, group]
        ksum[k] = total
        to_peers(
            lambda peer: remote(
                ksum.at[k], kall.at[k, me], ka_send.at[k], ka_recv.at[k], {"ctx": peer}
            )
        )
        kall[k, me] = total

        @pl.when(me < groups - 1)
        def _():
            drain(grx.at[k], g_recv.at[k])

        @pl.when(me == groups - 1)
        def _():
            grx[k] = jnp.zeros(grx.shape[1:], BF16)

        if k + 2 >= chunks:
            drain(srcv.at[k], src_send.at[k])
            drain(incv.at[k], inc_send.at[k])

        @pl.loop(0, groups)
        def _(group):
            for part in range(3):
                strip = part * groups + group
                fgb[strip, tokens:, :] = grx[k, strip].astype(F32)
                columns = pl.ds(column(part, group, k), LANES)
                total = None
                for j in range(taps):
                    term = kern[j : j + 1, columns] * fgb[strip, pl.ds(j, tokens), :]
                    total = term if total is None else total + term
                srcv[k, strip] = total.astype(BF16)
                pltpu.make_async_copy(
                    srcv.at[k, strip], igrad.at[:, columns], i_sem.at[k]
                ).start()

    for k in range(chunks):
        stage_a(k)
        if k > 0:
            stage_d(k - 1)
        stage_c(k)
    stage_d(chunks - 1)

    for k in range(chunks):
        drain(kall.at[k, pl.ds(0, groups - 1)], ka_recv.at[k])

        @pl.loop(0, groups)
        def _(group):
            for part in range(3):
                kgrad[:, pl.ds(column(part, group, k), LANES)] = kall[k, group, part, :taps, :]

        drain(srcv.at[k], i_sem.at[k])
        drain(srcv.at[k, pl.ds(0, groups)], o_sem.at[k])
        drain(gx.at[k, pl.ds(0, (groups - 1) * tokens), :], r_send.at[k])
        drain(kst.at[k, pl.ds(0, groups - 1)], ks_send.at[k])
        drain(kst.at[k, pl.ds(0, groups - 1)], ka_send.at[k])

        @pl.when(me < groups - 1)
        def _():
            drain(hst.at[k], h_send.at[k])

        @pl.when(me > 0)
        def _():
            drain(gst.at[k], g_send.at[k])


def on_device(sections, groups, acts, cots, kern, filt, skip):
    tokens, feats = acts.shape[1:]
    width = cots.shape[2]
    chans = width // groups
    chunks = chans // LANES
    length = filt.shape[2]
    taps = kern.shape[1]
    strips = 3 * groups
    vmem = pl.BlockSpec(memory_space=pltpu.VMEM)
    anywhere = pl.BlockSpec(memory_space=pl.ANY)
    dma = pltpu.SemaphoreType.DMA((chunks,))
    c4, s4, twist = make_tables(length)
    out, igrad, kgrad, fgrad, sgrad = pl.pallas_call(
        functools.partial(kernel, sections, groups, chunks),
        out_shape=(
            jax.ShapeDtypeStruct((tokens, width), BF16),
            jax.ShapeDtypeStruct((tokens, feats), BF16),
            jax.ShapeDtypeStruct((taps, feats), F32),
            jax.ShapeDtypeStruct((chans, length), F32),
            jax.ShapeDtypeStruct((1, chans), F32),
        ),
        in_specs=[anywhere, anywhere] + [vmem] * 6,
        out_specs=(anywhere, anywhere, vmem, vmem, vmem),
        scratch_shapes=[
            pltpu.VMEM((chunks, strips, tokens, LANES), BF16),
            pltpu.VMEM((chunks, groups, tokens, LANES), BF16),
            pltpu.VMEM((chunks, strips, HALO, LANES), BF16),
            pltpu.VMEM((chunks, strips, HALO, LANES), BF16),
            pltpu.VMEM((chunks, strips, HALO, LANES), BF16),
            pltpu.VMEM((chunks, strips, HALO, LANES), BF16),
            pltpu.VMEM((chunks, groups, tokens, 2 * LANES), BF16),
            pltpu.VMEM((chunks, length, 2 * LANES), BF16),
            pltpu.VMEM((chunks, groups, tokens, 2 * LANES), BF16),
            pltpu.VMEM((3, tokens + HALO, LANES), F32),
            pltpu.VMEM((strips, tokens + HALO, LANES), F32),
            pltpu.VMEM((2, chunks, length, LANES), BF16),
            pltpu.VMEM((2, length, 3 * LANES), BF16),
            pltpu.VMEM((chunks, groups, 3, 8, LANES), F32),
            pltpu.VMEM((chunks, groups, 3, 8, LANES), F32),
            pltpu.VMEM((chunks, 3, 8, LANES), F32),
            pltpu.VMEM((chunks, groups, 3, 8, LANES), F32),
        ]
        + [dma] * 18,
        compiler_params=pltpu.CompilerParams(
            collective_id=0, has_side_effects=True, vmem_limit_bytes=63 * 1024 * 1024
        ),
        cost_estimate=pl.CostEstimate(
            flops=2 * length * length * chans * 12, bytes_accessed=30_000_000, transcendentals=0
        ),
    )(acts[0], cots[0], kern[0], filt[0], skip, jnp.asarray(c4), jnp.asarray(s4), jnp.asarray(twist))
    return (out[None], igrad[None], kgrad[None], fgrad[None], sgrad)


def solution(mesh):
    return jax.shard_map(
        functools.partial(on_device, mesh.shape["section"], mesh.shape["ctx"]),
        mesh=mesh,
        in_specs=(
            P("section", "ctx", None),
            P("section", "ctx", None),
            P("section", None, None),
            P("section", "ctx", None),
            P("section", None),
        ),
        out_specs=(
            P("section", "ctx", None),
            P("section", "ctx", None),
            P("section", None, None),
            P("section", "ctx", None),
            P("section", "ctx"),
        ),
        check_vma=False,
    )
```

```python
import functools

import jax
import jax.numpy as jnp
import ml_dtypes
import numpy as np
from jax import lax
from jax.experimental import pallas as pl
from jax.experimental.pallas import tpu as pltpu
from jax.sharding import PartitionSpec as P

MESH = pl.DeviceIdType.MESH
LANES = 128
HALO = 16
F32 = jnp.float32
BF16 = jnp.bfloat16


def make_tables(length):
    half = 2 * np.arange(length, dtype=np.int64) + 1
    angle = (np.outer(half, half) % (8 * length)) * (2.0 * np.pi / (8 * length))
    phase = half * (np.pi / (4 * length))
    twist = np.stack([np.cos(phase), np.sin(phase)]).astype(np.float32)
    twist = np.ascontiguousarray(np.broadcast_to(twist[:, :, None], (2, length, LANES)))
    return (
        np.cos(angle).astype(ml_dtypes.bfloat16),
        np.sin(angle).astype(ml_dtypes.bfloat16),
        twist,
    )


def kernel(
    sections, groups, chunks,
    acts, cots, kern, filt, skip, c4, s4, twist,
    out, igrad, kgrad, fgrad, sgrad,
    srcv, incv, hst, hrx, gst, grx, stg, gx, rx, xf, fgb, fsp, prod, kst, krx, ksum, kall,
    src_send, src_recv, inc_send, inc_recv, h_send, h_recv, g_send, g_recv,
    x_send, x_recv, r_send, r_recv, ks_send, ks_recv, ka_send, ka_recv, o_sem, i_sem,
):
    sec = lax.axis_index("section")
    me = lax.axis_index("ctx")
    tokens, width = cots.shape
    chans = width // groups
    taps = kern.shape[0]
    length = c4.shape[0]
    rows_step = 256
    after_sec = lax.rem(sec + 1, sections)
    before_sec = lax.rem(sec + sections - 1, sections)

    barrier = pltpu.get_barrier_semaphore()
    pl.semaphore_signal(barrier, inc=1, device_id={"section": after_sec}, device_id_type=MESH)
    pl.semaphore_signal(barrier, inc=1, device_id={"section": before_sec}, device_id_type=MESH)
    for step in range(1, groups):
        pl.semaphore_signal(
            barrier, inc=1, device_id={"ctx": lax.rem(me + step, groups)}, device_id_type=MESH
        )
    pl.semaphore_wait(barrier, groups + 1)

    def column(part, group, k):
        return pl.multiple_of(part * width + group * chans + k * LANES, LANES)

    def remote(src, dst, send, recv, where):
        return pltpu.make_async_remote_copy(
            src_ref=src, dst_ref=dst, send_sem=send, recv_sem=recv,
            device_id=where, device_id_type=MESH,
        )

    def drain(ref, sem):
        pltpu.make_async_copy(ref, ref, sem).wait()

    def hand_on(k):
        def body(group, carry):
            for part in range(3):
                remote(
                    acts.at[:, pl.ds(column(part, group, k), LANES)],
                    srcv.at[k, part * groups + group],
                    src_send.at[k], src_recv.at[k], {"section": after_sec},
                ).start()
            remote(
                cots.at[:, pl.ds(column(0, group, k), LANES)],
                incv.at[k, group],
                inc_send.at[k], inc_recv.at[k], {"section": before_sec},
            ).start()
            return carry

        lax.fori_loop(0, groups, body, 0)

    def to_peers(make):
        def body(step, carry):
            make(lax.rem(me + step, groups)).start()
            return carry

        lax.fori_loop(1, groups, body, 0)

    def features(k, group):
        result = []
        for part in range(3):
            strip = part * groups + group
            xf[part, :HALO, :] = hrx[k, strip].astype(F32)
            xf[part, HALO:, :] = srcv[k, strip].astype(F32)
            columns = pl.ds(column(part, group, k), LANES)
            total = None
            for j in range(taps):
                term = kern[j, :, columns] * xf[part, pl.ds(HALO - j, tokens), :]
                total = term if total is None else total + term
            result.append(total)
        return result

    hand_on(0)

    @pl.loop(0, length // rows_step)
    def _(r):
        rows = pl.ds(pl.multiple_of(r * rows_step, rows_step), rows_step)
        dims = (((1,), (1,)), ((), ()))
        c = lax.dot_general(c4[rows, :], filt[...], dims, preferred_element_type=F32)
        s = lax.dot_general(s4[rows, :], filt[...], dims, preferred_element_type=F32)
        tc = twist[0, rows, :]
        ts = twist[1, rows, :]
        for k in range(chunks):
            ck = c[:, k * LANES : (k + 1) * LANES]
            sk = s[:, k * LANES : (k + 1) * LANES]
            fsp[0, k, rows, :] = (ck * tc + sk * ts).astype(BF16)
            fsp[1, k, rows, :] = (sk * tc - ck * ts).astype(BF16)

    def stage_a(k):
        drain(srcv.at[k], src_recv.at[k])
        drain(srcv.at[k], src_send.at[k])
        drain(incv.at[k], inc_send.at[k])
        if k + 1 < chunks:
            hand_on(k + 1)

        @pl.loop(0, 3 * groups)
        def _(strip):
            hst[k, strip] = srcv[k, strip, tokens - HALO :, :]

        @pl.when(me < groups - 1)
        def _():
            remote(hst.at[k], hrx.at[k], h_send.at[k], h_recv.at[k], {"ctx": me + 1}).start()

        drain(incv.at[k], inc_recv.at[k])

        @pl.when(me > 0)
        def _():
            drain(hrx.at[k], h_recv.at[k])

        @pl.when(me == 0)
        def _():
            hrx[k] = jnp.zeros(hrx.shape[1:], BF16)

        @pl.loop(0, groups)
        def _(group):
            query, keyed, value = features(k, group)
            stg[k, group, :, :LANES] = (keyed * value).astype(BF16)
            stg[k, group, :, LANES:] = (incv[k, group].astype(F32) * query).astype(BF16)

        mine = pl.ds(pl.multiple_of(me * tokens, tokens), tokens)
        to_peers(
            lambda peer: remote(
                stg.at[k, peer], gx.at[k, mine, :], x_send.at[k], x_recv.at[k], {"ctx": peer}
            )
        )
        gx[k, mine, :] = stg[k, me]

    def stage_c(k):
        drain(gx.at[k, pl.ds(0, (groups - 1) * tokens), :], x_recv.at[k])

        @pl.loop(0, length // rows_step)
        def _(r):
            rows = pl.ds(pl.multiple_of(r * rows_step, rows_step), rows_step)
            x = gx[k]
            c = jnp.dot(c4[rows, :], x, preferred_element_type=F32)
            s = jnp.dot(s4[rows, :], x, preferred_element_type=F32)
            cg, cm = c[:, :LANES], c[:, LANES:]
            sg, sm = s[:, :LANES], s[:, LANES:]
            fc = fsp[0, k, rows, :].astype(F32)
            fs = fsp[1, k, rows, :].astype(F32)
            prod[0, rows, :LANES] = (cg * fc - sg * fs).astype(BF16)
            prod[1, rows, :LANES] = (cg * fs + sg * fc).astype(BF16)
            prod[0, rows, LANES : 2 * LANES] = (cm * fc + sm * fs).astype(BF16)
            prod[1, rows, LANES : 2 * LANES] = (sm * fc - cm * fs).astype(BF16)
            uc = cm * cg + sm * sg
            us = sm * cg - cm * sg
            tc = twist[0, rows, :]
            ts = twist[1, rows, :]
            prod[0, rows, 2 * LANES :] = (uc * tc - us * ts).astype(BF16)
            prod[1, rows, 2 * LANES :] = (uc * ts + us * tc).astype(BF16)

        gain = skip[:, pl.ds(pl.multiple_of(me * chans + k * LANES, LANES), LANES)]

        def back(r, total):
            start = pl.multiple_of(r * rows_step, rows_step)
            rows = pl.ds(start, rows_step)
            y = jnp.dot(c4[rows, :], prod[0], preferred_element_type=F32)
            y = y + jnp.dot(s4[rows, :], prod[1], preferred_element_type=F32)
            y = y * (1.0 / length)
            gated = gx[k, rows, :LANES].astype(F32)
            grad = gx[k, rows, LANES:].astype(F32)
            gx[k, rows, :LANES] = y[:, :LANES].astype(BF16)
            gx[k, rows, LANES:] = (y[:, LANES : 2 * LANES] + gain * grad).astype(BF16)
            fgrad[k * LANES : (k + 1) * LANES, rows] = y[:, 2 * LANES :].T
            return total + jnp.sum(gated * grad, axis=0, keepdims=True)

        sgrad[:, k * LANES : (k + 1) * LANES] = lax.fori_loop(
            0, length // rows_step, back, jnp.zeros((1, LANES), F32)
        )
        to_peers(
            lambda peer: remote(
                gx.at[k, pl.ds(pl.multiple_of(peer * tokens, tokens), tokens), :],
                rx.at[k, me],
                r_send.at[k], r_recv.at[k], {"ctx": peer},
            )
        )
        rx[k, me] = gx[k, pl.ds(pl.multiple_of(me * tokens, tokens), tokens), :]

    def stage_d(k):
        drain(rx.at[k, pl.ds(0, groups - 1)], r_recv.at[k])
        drain(stg.at[k, pl.ds(0, groups - 1)], x_send.at[k])

        @pl.loop(0, groups)
        def _(group):
            query, keyed, value = features(k, group)
            gain = skip[:, pl.ds(column(0, group, k), LANES)]
            mixed = rx[k, group, :, :LANES].astype(F32)
            through = rx[k, group, :, LANES:].astype(F32)
            inner = mixed + gain * stg[k, group, :, :LANES].astype(F32)
            stg[k, group, :, :LANES] = (query * inner).astype(BF16)
            pltpu.make_async_copy(
                stg.at[k, group, :, pl.ds(0, LANES)],
                out.at[:, pl.ds(column(0, group, k), LANES)],
                o_sem.at[k],
            ).start()
            grads = (incv[k, group].astype(F32) * inner, through * value, through * keyed)
            for part in range(3):
                strip = part * groups + group
                grad = grads[part]
                fgb[strip, :tokens, :] = grad
                gst[k, strip] = grad[:HALO].astype(BF16)
                for j in range(taps):
                    kst[k, group, part, j : j + 1, :] = jnp.sum(
                        grad * xf[part, pl.ds(HALO - j, tokens), :], axis=0, keepdims=True
                    )
                kst[k, group, part, taps:, :] = jnp.zeros((8 - taps, LANES), F32)

        @pl.when(me > 0)
        def _():
            remote(gst.at[k], grx.at[k], g_send.at[k], g_recv.at[k], {"ctx": me - 1}).start()

        to_peers(
            lambda peer: remote(
                kst.at[k, peer], krx.at[k, me], ks_send.at[k], ks_recv.at[k], {"ctx": peer}
            )
        )
        krx[k, me] = kst[k, me]

    def stage_e(k):
        drain(krx.at[k, pl.ds(0, groups - 1)], ks_recv.at[k])
        total = krx[k, 0]
        for group in range(1, groups):
            total = total + krx[k, group]
        ksum[k] = total
        to_peers(
            lambda peer: remote(
                ksum.at[k], kall.at[k, me], ka_send.at[k], ka_recv.at[k], {"ctx": peer}
            )
        )
        kall[k, me] = total

        @pl.when(me < groups - 1)
        def _():
            drain(grx.at[k], g_recv.at[k])

        @pl.when(me == groups - 1)
        def _():
            grx[k] = jnp.zeros(grx.shape[1:], BF16)

        @pl.loop(0, groups)
        def _(group):
            for part in range(3):
                strip = part * groups + group
                fgb[strip, tokens:, :] = grx[k, strip].astype(F32)
                columns = pl.ds(column(part, group, k), LANES)
                total = None
                for j in range(taps):
                    term = kern[j, :, columns] * fgb[strip, pl.ds(j, tokens), :]
                    total = term if total is None else total + term
                srcv[k, strip] = total.astype(BF16)
                pltpu.make_async_copy(
                    srcv.at[k, strip], igrad.at[:, columns], i_sem.at[k]
                ).start()

    plan = []
    for k in range(chunks):
        plan.append((stage_a, k))
        if k == 0:
            plan.append((stage_c, 0))
        elif k == 1:
            plan.append((stage_d, 0))
        elif k == 2:
            plan += [(stage_e, 0), (stage_c, 1)]
        else:
            plan += [(stage_c, k - 1), (stage_d, k - 2), (stage_e, k - 2)]
    for k in range(chunks):
        if (stage_c, k) not in plan:
            plan.append((stage_c, k))
    for k in range(chunks):
        for stage in (stage_d, stage_e):
            if (stage, k) not in plan:
                plan.append((stage, k))
    for stage, k in plan:
        stage(k)

    for k in range(chunks):
        drain(kall.at[k, pl.ds(0, groups - 1)], ka_recv.at[k])

        @pl.loop(0, groups)
        def _(group):
            for part in range(3):
                columns = pl.ds(column(part, group, k), LANES)
                for j in range(taps):
                    kgrad[j, :, columns] = kall[k, group, part, j : j + 1, :]

        drain(srcv.at[k], i_sem.at[k])
        drain(srcv.at[k, pl.ds(0, groups)], o_sem.at[k])
        drain(gx.at[k, pl.ds(0, (groups - 1) * tokens), :], r_send.at[k])
        drain(kst.at[k, pl.ds(0, groups - 1)], ks_send.at[k])
        drain(kst.at[k, pl.ds(0, groups - 1)], ka_send.at[k])

        @pl.when(me < groups - 1)
        def _():
            drain(hst.at[k], h_send.at[k])

        @pl.when(me > 0)
        def _():
            drain(gst.at[k], g_send.at[k])


def copy_kernel(*refs):
    count = len(refs) // 2
    sems = refs[-1]
    started = []
    for i in range(count):
        src, dst = refs[i], refs[count + i]
        parts = 4 if src.shape[0] % 64 == 0 else 1
        rows = src.shape[0] // parts
        for part in range(parts):
            here = pl.ds(part * rows, rows)
            copy = pltpu.make_async_copy(src.at[here], dst.at[here], sems.at[i, part])
            copy.start()
            started.append(copy)
    for copy in started:
        copy.wait()


def copied(arrays):
    anywhere = pl.BlockSpec(memory_space=pl.ANY)
    return pl.pallas_call(
        copy_kernel,
        out_shape=tuple(jax.ShapeDtypeStruct(a.shape, a.dtype) for a in arrays),
        in_specs=[anywhere] * len(arrays),
        out_specs=(anywhere,) * len(arrays),
        scratch_shapes=[pltpu.SemaphoreType.DMA((len(arrays), 4))],
        compiler_params=pltpu.CompilerParams(vmem_limit_bytes=63 * 1024 * 1024),
    )(*arrays)


def on_device(sections, groups, acts, cots, kern, filt, skip):
    tokens, feats = acts.shape[1:]
    width = cots.shape[2]
    chans = width // groups
    chunks = chans // LANES
    length = filt.shape[2]
    taps = kern.shape[1]
    strips = 3 * groups
    vmem = pl.BlockSpec(memory_space=pltpu.VMEM)
    anywhere = pl.BlockSpec(memory_space=pl.ANY)
    dma = pltpu.SemaphoreType.DMA((chunks,))
    c4, s4, twist = make_tables(length)
    out, igrad, kgrad, fgrad, sgrad = pl.pallas_call(
        functools.partial(kernel, sections, groups, chunks),
        out_shape=(
            jax.ShapeDtypeStruct((tokens, width), BF16),
            jax.ShapeDtypeStruct((tokens, feats), BF16),
            jax.ShapeDtypeStruct((taps, 1, feats), F32),
            jax.ShapeDtypeStruct((chans, length), F32),
            jax.ShapeDtypeStruct((1, chans), F32),
        ),
        in_specs=[anywhere, anywhere] + [vmem] * 6,
        out_specs=(anywhere, anywhere, vmem, vmem, vmem),
        scratch_shapes=[
            pltpu.VMEM((chunks, strips, tokens, LANES), BF16),
            pltpu.VMEM((chunks, groups, tokens, LANES), BF16),
            pltpu.VMEM((chunks, strips, HALO, LANES), BF16),
            pltpu.VMEM((chunks, strips, HALO, LANES), BF16),
            pltpu.VMEM((chunks, strips, HALO, LANES), BF16),
            pltpu.VMEM((chunks, strips, HALO, LANES), BF16),
            pltpu.VMEM((chunks, groups, tokens, 2 * LANES), BF16),
            pltpu.VMEM((chunks, length, 2 * LANES), BF16),
            pltpu.VMEM((chunks, groups, tokens, 2 * LANES), BF16),
            pltpu.VMEM((3, tokens + HALO, LANES), F32),
            pltpu.VMEM((strips, tokens + HALO, LANES), F32),
            pltpu.VMEM((2, chunks, length, LANES), BF16),
            pltpu.VMEM((2, length, 3 * LANES), BF16),
            pltpu.VMEM((chunks, groups, 3, 8, LANES), F32),
            pltpu.VMEM((chunks, groups, 3, 8, LANES), F32),
            pltpu.VMEM((chunks, 3, 8, LANES), F32),
            pltpu.VMEM((chunks, groups, 3, 8, LANES), F32),
        ]
        + [dma] * 18,
        compiler_params=pltpu.CompilerParams(
            collective_id=0, has_side_effects=True, vmem_limit_bytes=63 * 1024 * 1024
        ),
        cost_estimate=pl.CostEstimate(
            flops=2 * length * length * chans * 12, bytes_accessed=30_000_000, transcendentals=0
        ),
    )(acts[0], cots[0], kern.transpose(1, 0, 2), filt[0], skip, jnp.asarray(c4), jnp.asarray(s4), jnp.asarray(twist))
    out, igrad, kgrad, fgrad = copied((out, igrad, kgrad, fgrad))
    return (out[None], igrad[None], kgrad.transpose(1, 0, 2), fgrad[None], sgrad)


def solution(mesh):
    return jax.shard_map(
        functools.partial(on_device, mesh.shape["section"], mesh.shape["ctx"]),
        mesh=mesh,
        in_specs=(
            P("section", "ctx", None),
            P("section", "ctx", None),
            P("section", None, None),
            P("section", "ctx", None),
            P("section", None),
        ),
        out_specs=(
            P("section", "ctx", None),
            P("section", "ctx", None),
            P("section", None, None),
            P("section", "ctx", None),
            P("section", "ctx"),
        ),
        check_vma=False,
    )
```

```python
import functools

import jax
import jax.numpy as jnp
import ml_dtypes
import numpy as np
from jax import lax
from jax.experimental import pallas as pl
from jax.experimental.pallas import tpu as pltpu
from jax.sharding import PartitionSpec as P

MESH = pl.DeviceIdType.MESH
LANES = 128
HALO = 16
F32 = jnp.float32
BF16 = jnp.bfloat16


def make_tables(length):
    half = 2 * np.arange(length, dtype=np.int64) + 1
    angle = (np.outer(half, half) % (8 * length)) * (2.0 * np.pi / (8 * length))
    phase = half * (np.pi / (4 * length))
    twist = np.stack([np.cos(phase), np.sin(phase)]).astype(np.float32)
    twist = np.ascontiguousarray(np.broadcast_to(twist[:, :, None], (2, length, LANES)))
    return (
        np.cos(angle).astype(ml_dtypes.bfloat16),
        np.sin(angle).astype(ml_dtypes.bfloat16),
        twist,
    )


def kernel(
    sections, groups, chunks,
    acts, cots, kern, filt, skip, c4, s4, twist,
    out, igrad, kgrad, fgrad, sgrad,
    srcv, incv, hst, hrx, gst, grx, stg, gx, rx, xf, fgb, fsp, prod, kst, krx, ksum, kall,
    src_send, src_recv, inc_send, inc_recv, h_send, h_recv, g_send, g_recv,
    x_send, x_recv, r_send, r_recv, ks_send, ks_recv, ka_send, ka_recv, o_sem, i_sem,
):
    sec = lax.axis_index("section")
    me = lax.axis_index("ctx")
    tokens, width = cots.shape
    chans = width // groups
    taps = kern.shape[0]
    length = c4.shape[0]
    rows_step = 256
    after_sec = lax.rem(sec + 1, sections)
    before_sec = lax.rem(sec + sections - 1, sections)

    barrier = pltpu.get_barrier_semaphore()
    pl.semaphore_signal(barrier, inc=1, device_id={"section": after_sec}, device_id_type=MESH)
    pl.semaphore_signal(barrier, inc=1, device_id={"section": before_sec}, device_id_type=MESH)
    for step in range(1, groups):
        pl.semaphore_signal(
            barrier, inc=1, device_id={"ctx": lax.rem(me + step, groups)}, device_id_type=MESH
        )
    pl.semaphore_wait(barrier, groups + 1)

    def column(part, group, k):
        return pl.multiple_of(part * width + group * chans + k * LANES, LANES)

    def remote(src, dst, send, recv, where):
        return pltpu.make_async_remote_copy(
            src_ref=src, dst_ref=dst, send_sem=send, recv_sem=recv,
            device_id=where, device_id_type=MESH,
        )

    def drain(ref, sem):
        pltpu.make_async_copy(ref, ref, sem).wait()

    def hand_on(k):
        def body(group, carry):
            for part in range(3):
                remote(
                    acts.at[:, pl.ds(column(part, group, k), LANES)],
                    srcv.at[k, part * groups + group],
                    src_send.at[k], src_recv.at[k], {"section": after_sec},
                ).start()
            remote(
                cots.at[:, pl.ds(column(0, group, k), LANES)],
                incv.at[k, group],
                inc_send.at[k], inc_recv.at[k], {"section": before_sec},
            ).start()
            return carry

        lax.fori_loop(0, groups, body, 0)

    def to_peers(make):
        def body(step, carry):
            make(lax.rem(me + step, groups)).start()
            return carry

        lax.fori_loop(1, groups, body, 0)

    def features(k, group):
        result = []
        for part in range(3):
            strip = part * groups + group
            xf[part, :HALO, :] = hrx[k, strip].astype(F32)
            xf[part, HALO:, :] = srcv[k, strip].astype(F32)
            columns = pl.ds(column(part, group, k), LANES)
            total = None
            for j in range(taps):
                term = kern[j, :, columns] * xf[part, pl.ds(HALO - j, tokens), :]
                total = term if total is None else total + term
            result.append(total)
        return result

    hand_on(0)

    @pl.loop(0, length // rows_step)
    def _(r):
        rows = pl.ds(pl.multiple_of(r * rows_step, rows_step), rows_step)
        dims = (((1,), (1,)), ((), ()))
        c = lax.dot_general(c4[rows, :], filt[...], dims, preferred_element_type=F32)
        s = lax.dot_general(s4[rows, :], filt[...], dims, preferred_element_type=F32)
        tc = twist[0, rows, :]
        ts = twist[1, rows, :]
        for k in range(chunks):
            ck = c[:, k * LANES : (k + 1) * LANES]
            sk = s[:, k * LANES : (k + 1) * LANES]
            fsp[0, k, rows, :] = (ck * tc + sk * ts).astype(BF16)
            fsp[1, k, rows, :] = (sk * tc - ck * ts).astype(BF16)

    def stage_a(k):
        drain(srcv.at[k], src_recv.at[k])
        drain(srcv.at[k], src_send.at[k])
        drain(incv.at[k], inc_send.at[k])
        if k + 1 < chunks:
            hand_on(k + 1)

        @pl.loop(0, 3 * groups)
        def _(strip):
            hst[k, strip] = srcv[k, strip, tokens - HALO :, :]

        @pl.when(me < groups - 1)
        def _():
            remote(hst.at[k], hrx.at[k], h_send.at[k], h_recv.at[k], {"ctx": me + 1}).start()

        drain(incv.at[k], inc_recv.at[k])

        @pl.when(me > 0)
        def _():
            drain(hrx.at[k], h_recv.at[k])

        @pl.when(me == 0)
        def _():
            hrx[k] = jnp.zeros(hrx.shape[1:], BF16)

        @pl.loop(0, groups)
        def _(group):
            query, keyed, value = features(k, group)
            stg[k, group, :, :LANES] = (keyed * value).astype(BF16)
            stg[k, group, :, LANES:] = (incv[k, group].astype(F32) * query).astype(BF16)

        mine = pl.ds(pl.multiple_of(me * tokens, tokens), tokens)
        to_peers(
            lambda peer: remote(
                stg.at[k, peer], gx.at[k, mine, :], x_send.at[k], x_recv.at[k], {"ctx": peer}
            )
        )
        gx[k, mine, :] = stg[k, me]

    def stage_c(k):
        drain(gx.at[k, pl.ds(0, (groups - 1) * tokens), :], x_recv.at[k])

        @pl.loop(0, length // rows_step)
        def _(r):
            rows = pl.ds(pl.multiple_of(r * rows_step, rows_step), rows_step)
            x = gx[k]
            c = jnp.dot(c4[rows, :], x, preferred_element_type=F32)
            s = jnp.dot(s4[rows, :], x, preferred_element_type=F32)
            cg, cm = c[:, :LANES], c[:, LANES:]
            sg, sm = s[:, :LANES], s[:, LANES:]
            fc = fsp[0, k, rows, :].astype(F32)
            fs = fsp[1, k, rows, :].astype(F32)
            prod[0, rows, :LANES] = (cg * fc - sg * fs).astype(BF16)
            prod[1, rows, :LANES] = (cg * fs + sg * fc).astype(BF16)
            prod[0, rows, LANES : 2 * LANES] = (cm * fc + sm * fs).astype(BF16)
            prod[1, rows, LANES : 2 * LANES] = (sm * fc - cm * fs).astype(BF16)
            uc = cm * cg + sm * sg
            us = sm * cg - cm * sg
            tc = twist[0, rows, :]
            ts = twist[1, rows, :]
            prod[0, rows, 2 * LANES :] = (uc * tc - us * ts).astype(BF16)
            prod[1, rows, 2 * LANES :] = (uc * ts + us * tc).astype(BF16)

        gain = skip[:, pl.ds(pl.multiple_of(me * chans + k * LANES, LANES), LANES)]

        def back(r, total):
            start = pl.multiple_of(r * rows_step, rows_step)
            rows = pl.ds(start, rows_step)
            y = jnp.dot(c4[rows, :], prod[0], preferred_element_type=F32)
            y = y + jnp.dot(s4[rows, :], prod[1], preferred_element_type=F32)
            y = y * (1.0 / length)
            gated = gx[k, rows, :LANES].astype(F32)
            grad = gx[k, rows, LANES:].astype(F32)
            gx[k, rows, :LANES] = y[:, :LANES].astype(BF16)
            gx[k, rows, LANES:] = (y[:, LANES : 2 * LANES] + gain * grad).astype(BF16)
            fgrad[k * LANES : (k + 1) * LANES, rows] = y[:, 2 * LANES :].T
            return total + jnp.sum(gated * grad, axis=0, keepdims=True)

        sgrad[:, k * LANES : (k + 1) * LANES] = lax.fori_loop(
            0, length // rows_step, back, jnp.zeros((1, LANES), F32)
        )
        to_peers(
            lambda peer: remote(
                gx.at[k, pl.ds(pl.multiple_of(peer * tokens, tokens), tokens), :],
                rx.at[k, me],
                r_send.at[k], r_recv.at[k], {"ctx": peer},
            )
        )
        rx[k, me] = gx[k, pl.ds(pl.multiple_of(me * tokens, tokens), tokens), :]

    def stage_d(k):
        drain(rx.at[k, pl.ds(0, groups - 1)], r_recv.at[k])
        drain(stg.at[k, pl.ds(0, groups - 1)], x_send.at[k])

        @pl.loop(0, groups)
        def _(group):
            query, keyed, value = features(k, group)
            gain = skip[:, pl.ds(column(0, group, k), LANES)]
            mixed = rx[k, group, :, :LANES].astype(F32)
            through = rx[k, group, :, LANES:].astype(F32)
            inner = mixed + gain * stg[k, group, :, :LANES].astype(F32)
            stg[k, group, :, :LANES] = (query * inner).astype(BF16)
            pltpu.make_async_copy(
                stg.at[k, group, :, pl.ds(0, LANES)],
                out.at[:, pl.ds(column(0, group, k), LANES)],
                o_sem.at[k],
            ).start()
            grads = (incv[k, group].astype(F32) * inner, through * value, through * keyed)
            for part in range(3):
                strip = part * groups + group
                grad = grads[part]
                fgb[strip, :tokens, :] = grad
                gst[k, strip] = grad[:HALO].astype(BF16)
                for j in range(taps):
                    kst[k, group, part, j : j + 1, :] = jnp.sum(
                        grad * xf[part, pl.ds(HALO - j, tokens), :], axis=0, keepdims=True
                    )
                kst[k, group, part, taps:, :] = jnp.zeros((8 - taps, LANES), F32)

        @pl.when(me > 0)
        def _():
            remote(gst.at[k], grx.at[k], g_send.at[k], g_recv.at[k], {"ctx": me - 1}).start()

        to_peers(
            lambda peer: remote(
                kst.at[k, peer], krx.at[k, me], ks_send.at[k], ks_recv.at[k], {"ctx": peer}
            )
        )
        krx[k, me] = kst[k, me]

    def stage_e(k):
        drain(krx.at[k, pl.ds(0, groups - 1)], ks_recv.at[k])
        total = krx[k, 0]
        for group in range(1, groups):
            total = total + krx[k, group]
        ksum[k] = total
        to_peers(
            lambda peer: remote(
                ksum.at[k], kall.at[k, me], ka_send.at[k], ka_recv.at[k], {"ctx": peer}
            )
        )
        kall[k, me] = total

        @pl.when(me < groups - 1)
        def _():
            drain(grx.at[k], g_recv.at[k])

        @pl.when(me == groups - 1)
        def _():
            grx[k] = jnp.zeros(grx.shape[1:], BF16)

        @pl.loop(0, groups)
        def _(group):
            for part in range(3):
                strip = part * groups + group
                fgb[strip, tokens:, :] = grx[k, strip].astype(F32)
                columns = pl.ds(column(part, group, k), LANES)
                total = None
                for j in range(taps):
                    term = kern[j, :, columns] * fgb[strip, pl.ds(j, tokens), :]
                    total = term if total is None else total + term
                srcv[k, strip] = total.astype(BF16)
                pltpu.make_async_copy(
                    srcv.at[k, strip], igrad.at[:, columns], i_sem.at[k]
                ).start()

    plan = []
    for k in range(chunks):
        plan.append((stage_a, k))
        if k == 0:
            plan.append((stage_c, 0))
        elif k == 1:
            plan.append((stage_d, 0))
        elif k == 2:
            plan += [(stage_e, 0), (stage_c, 1)]
        else:
            plan += [(stage_c, k - 1), (stage_d, k - 2), (stage_e, k - 2)]
    for k in range(chunks):
        if (stage_c, k) not in plan:
            plan.append((stage_c, k))
    for k in range(chunks):
        for stage in (stage_d, stage_e):
            if (stage, k) not in plan:
                plan.append((stage, k))
    for stage, k in plan:
        stage(k)

    for k in range(chunks):
        drain(kall.at[k, pl.ds(0, groups - 1)], ka_recv.at[k])

        @pl.loop(0, groups)
        def _(group):
            for part in range(3):
                columns = pl.ds(column(part, group, k), LANES)
                for j in range(taps):
                    kgrad[j, :, columns] = kall[k, group, part, j : j + 1, :]

        drain(srcv.at[k], i_sem.at[k])
        drain(srcv.at[k, pl.ds(0, groups)], o_sem.at[k])
        drain(gx.at[k, pl.ds(0, (groups - 1) * tokens), :], r_send.at[k])
        drain(kst.at[k, pl.ds(0, groups - 1)], ks_send.at[k])
        drain(kst.at[k, pl.ds(0, groups - 1)], ka_send.at[k])

        @pl.when(me < groups - 1)
        def _():
            drain(hst.at[k], h_send.at[k])

        @pl.when(me > 0)
        def _():
            drain(gst.at[k], g_send.at[k])


def on_device(sections, groups, acts, cots, kern, filt, skip):
    tokens, feats = acts.shape[1:]
    width = cots.shape[2]
    chans = width // groups
    chunks = chans // LANES
    length = filt.shape[2]
    taps = kern.shape[1]
    strips = 3 * groups
    vmem = pl.BlockSpec(memory_space=pltpu.VMEM)
    anywhere = pl.BlockSpec(memory_space=pl.ANY)
    dma = pltpu.SemaphoreType.DMA((chunks,))
    c4, s4, twist = make_tables(length)
    out, igrad, kgrad, fgrad, sgrad = pl.pallas_call(
        functools.partial(kernel, sections, groups, chunks),
        out_shape=(
            jax.ShapeDtypeStruct((tokens, width), BF16),
            jax.ShapeDtypeStruct((tokens, feats), BF16),
            jax.ShapeDtypeStruct((taps, 1, feats), F32),
            jax.ShapeDtypeStruct((chans, length), F32),
            jax.ShapeDtypeStruct((1, chans), F32),
        ),
        in_specs=[anywhere, anywhere] + [vmem] * 6,
        out_specs=(anywhere, anywhere, vmem, vmem, vmem),
        scratch_shapes=[
            pltpu.VMEM((chunks, strips, tokens, LANES), BF16),
            pltpu.VMEM((chunks, groups, tokens, LANES), BF16),
            pltpu.VMEM((chunks, strips, HALO, LANES), BF16),
            pltpu.VMEM((chunks, strips, HALO, LANES), BF16),
            pltpu.VMEM((chunks, strips, HALO, LANES), BF16),
            pltpu.VMEM((chunks, strips, HALO, LANES), BF16),
            pltpu.VMEM((chunks, groups, tokens, 2 * LANES), BF16),
            pltpu.VMEM((chunks, length, 2 * LANES), BF16),
            pltpu.VMEM((chunks, groups, tokens, 2 * LANES), BF16),
            pltpu.VMEM((3, tokens + HALO, LANES), F32),
            pltpu.VMEM((strips, tokens + HALO, LANES), F32),
            pltpu.VMEM((2, chunks, length, LANES), BF16),
            pltpu.VMEM((2, length, 3 * LANES), BF16),
            pltpu.VMEM((chunks, groups, 3, 8, LANES), F32),
            pltpu.VMEM((chunks, groups, 3, 8, LANES), F32),
            pltpu.VMEM((chunks, 3, 8, LANES), F32),
            pltpu.VMEM((chunks, groups, 3, 8, LANES), F32),
        ]
        + [dma] * 18,
        compiler_params=pltpu.CompilerParams(
            collective_id=0, has_side_effects=True, vmem_limit_bytes=63 * 1024 * 1024
        ),
        cost_estimate=pl.CostEstimate(
            flops=2 * length * length * chans * 12, bytes_accessed=30_000_000, transcendentals=0
        ),
    )(acts[0], cots[0], kern.transpose(1, 0, 2), filt[0], skip, jnp.asarray(c4), jnp.asarray(s4), jnp.asarray(twist))
    return (out[None], igrad[None], kgrad.transpose(1, 0, 2), fgrad[None], sgrad)


def solution(mesh):
    return jax.shard_map(
        functools.partial(on_device, mesh.shape["section"], mesh.shape["ctx"]),
        mesh=mesh,
        in_specs=(
            P("section", "ctx", None),
            P("section", "ctx", None),
            P("section", None, None),
            P("section", "ctx", None),
            P("section", None),
        ),
        out_specs=(
            P("section", "ctx", None),
            P("section", "ctx", None),
            P("section", None, None),
            P("section", "ctx", None),
            P("section", "ctx"),
        ),
        check_vma=False,
    )
```
